512 devices in a mesh: dp: 4 (over x), ctx: 8 (over y, core), expert: 16 (over z).
Axes of the slice: x: 4, y: 4, z: 16, core: 2. Of those that a mesh axis runs over, the one named last changes fastest.
Arguments:
- tokens: bfloat16 [65536, 2048], P(('dp', 'ctx', 'expert')), parts along dimension 0, may hold values from -6 to 6
- token_tangent: bfloat16 [65536, 2048], P(('dp', 'ctx', 'expert')), parts along dimension 0, may hold values from -6 to 6
- mod_scale: float32 [8192], P('dp'), parts along dimension 0, may hold values from -1.5 to 1.5
- mod_shift: float32 [8192], P('dp'), parts along dimension 0, may hold values from -1.5 to 1.5
- scale_tangent: float32 [8192], P('dp'), parts along dimension 0, may hold values from -3 to 3
- shift_tangent: float32 [8192], P('dp'), parts along dimension 0, may hold values from -3 to 3
- out_gate: float32 [8192], P('dp'), parts along dimension 0, may hold values from 0.5 to 2
- out_gate_tangent: float32 [8192], P('dp'), parts along dimension 0, may hold values from -3 to 3
- routes: int32 [65536, 2], P(('dp', 'ctx', 'expert')), parts along dimension 0, may hold values from 0 to 15, all different within a row; in each aligned block of 128 rows (0 to 127, 128 to 255, ...) at most 32 rows name the same one
- router_gates: float32 [65536, 2], P(('dp', 'ctx', 'expert')), parts along dimension 0, may hold values from 0.05 to 0.95
- router_tangents: float32 [65536, 2], P(('dp', 'ctx', 'expert')), parts along dimension 0, may hold values from -3 to 3
- gate_weight: bfloat16 [16, 2048, 512], P('expert', 'ctx'), may hold values from -0.125 to 0.125
- up_weight: bfloat16 [16, 2048, 512], P('expert', 'ctx'), may hold values from -0.125 to 0.125
- down_weight: bfloat16 [16, 2048, 512], P('expert', 'ctx'), may hold values from -0.25 to 0.25
Outputs:
- mixed: bfloat16 [65536, 2048], P(('dp', 'ctx', 'expert')), parts along dimension 0
- mixed_tangent: bfloat16 [65536, 2048], P(('dp', 'ctx', 'expert')), parts along dimension 0
The draws below stay inside these ranges and needn't reach their ends.
There are 4 independent parts, one for each index of `dp`. The reference program is written for one: setup_inputs(seed, part) draws one part's arguments, and reference() takes and returns one part's arrays. A program takes and returns all parts, laid end to end along the dimension named above; an argument that names none is the same for every part. Nothing has to cross between parts.
Inputs may be any that keep to these rules, and one draw needn't show every extreme that they name: `routes`: among the rows of one device no expert is named by more than 32 rows, a bound that some block reaches.
All inputs are finite; a program needn't handle non-finite values.
Results may differ from the reference program's by a relative error of at most 0.0059.
Values may be sent and summed in bfloat16 or wider, within the bound.
A program may use at most 64 MiB of HBM per device.

```python
import math
import jax
import jax.numpy as jnp
import numpy as np
from jax import lax

D = 2048
FF = 512
TOK_DEV = 128
EXPERTS = 16
CAP = 32
TOKENS = 16384


def shared_rows(key, lowest, highest):
    values = jax.random.normal(key, (TOKENS, D), jnp.float32)
    scales = jax.random.uniform(jax.random.fold_in(key, 1), (TOKENS, 1), jnp.float32, lowest, highest)
    return values * scales


def draw_tokens(key, part):
    values = shared_rows(key, 1.0, 1.0)
    return jnp.clip(values, -6.0, 6.0).astype(jnp.bfloat16)


def draw_token_tangent(key, part):
    values = shared_rows(key, 1.0, 1.0)
    key = jax.random.fold_in(key, 23)
    factor = jax.random.uniform(jax.random.fold_in(key, 1), (TOKENS, 1), jnp.float32, -1.5, 1.5)
    noise = jax.random.normal(jax.random.fold_in(key, 2), (TOKENS, D), jnp.float32)
    return jnp.clip(factor * values + noise, -6.0, 6.0).astype(jnp.bfloat16)


def levels(key, shape, split, smallest, high):
    def one(axis_at, shards_of):
        heights = jax.random.uniform(jax.random.fold_in(jax.random.fold_in(key, 6), axis_at), (shards_of,), jnp.float32, smallest / len(split), high / len(split))
        return jnp.repeat(jnp.exp(heights), shape[axis_at] // shards_of).reshape((-1,) + (1,) * (len(shape) - axis_at - 1))

    factor_of = one(*split[0])
    for cut in split[1:]:
        factor_of = factor_of * one(*cut)
    return factor_of


def shared_out(key, own, number, rows, amount, top, reach, skew):
    order = jax.random.permutation(key, amount)
    packed, ordinary = shares(amount, rows * top, reach, skew, True), shares(amount, rows * top, reach, skew, False)
    places = jnp.arange(amount)

    def named(tallies, turn):
        used = int((tallies > 0).sum())
        fixed = max(1, used // 4)
        shifted = fixed + (places - fixed + turn * (used - fixed)) % max(1, amount - fixed)
        return jnp.zeros((amount,), jnp.int32).at[order[jnp.where(places < fixed, places, shifted)]].set(jnp.asarray(tallies, jnp.int32))

    tallies = jnp.where(number % 4 == 0, named(packed, number // 4), named(ordinary, number - number // 4 - 1))
    mixed = jax.random.permutation(jax.random.fold_in(own, 3), amount)
    source_of, taker = mixed[0:amount // 2 * 2:2], mixed[1:amount // 2 * 2:2]
    margin = jnp.minimum(tallies[source_of] - 1, reach - tallies[taker]) // 2
    margin = jnp.where((source_of == order[0]) | (taker == order[0]) | (tallies[taker] == 0), 0, jnp.maximum(margin, 0))
    shifted = jax.random.randint(jax.random.fold_in(own, 4), (amount // 2,), 0, 1 << 20) % (margin + 1)
    tallies = tallies.at[source_of].add(-shifted).at[taker].add(shifted)
    members = jnp.searchsorted(jnp.cumsum(tallies), jnp.arange(rows * top), side="right").astype(jnp.int32)
    listing = members.reshape(top, rows).T
    listing = listing[jax.random.permutation(jax.random.fold_in(own, 1), rows)]
    turn = jax.random.randint(jax.random.fold_in(own, 2), (rows, 1), 0, top)
    return jnp.take_along_axis(listing, (jnp.arange(top)[None, :] + turn) % top, axis=1)


def shares(number_of, total, reach, lean, full):
    weights = [(1 << 20) // math.isqrt(standing ** lean) + 1 for standing in range(1, number_of + 1)]
    largest = reach if full else min(reach, max(-(-total // number_of), total * weights[0] // sum(weights)))
    least = 1 if total - largest >= number_of - 1 else 0
    counts, surplus = [largest] + [least] * (number_of - 1), total - largest - least * (number_of - 1)
    while surplus > 0:
        free = [i for i in range(1, number_of) if counts[i] < largest] or [i for i in range(1, number_of) if counts[i] < reach]
        pool, remaining = sum([weights[i] for i in free]), surplus
        for i in free:
            more = min(reach - counts[i], max(1, remaining * weights[i] // pool), surplus)
            counts[i] = counts[i] + more
            surplus = surplus - more
    return np.array(counts)


def bell_draw(key, extent, deviation, most, pieces=(), held_as=jnp.bfloat16):
    values = jax.random.normal(key, extent, jnp.float32) * deviation
    if len(pieces) > 0:
        values = levels(key, extent, pieces, -0.22, 0.18) * values
    return jnp.clip(values, min=-most, max=most).astype(held_as)


def setup_inputs(seed: int = 0, part: int = 0) -> dict:
    keys = jax.random.split(jax.random.key(seed), 15)
    own_keys = jax.random.split(jax.random.fold_in(keys[14], part), 15)
    tokens = draw_tokens(jax.random.fold_in(jax.random.fold_in(keys[14], part), 71), part)
    token_tangent = draw_token_tangent(jax.random.fold_in(jax.random.fold_in(keys[14], part), 71), part)
    mod_scale = bell_draw(own_keys[2], (D,), 0.3, 1.5, (), jnp.float32)
    mod_shift = bell_draw(own_keys[3], (D,), 0.3, 1.5, (), jnp.float32)
    scale_tangent = bell_draw(own_keys[4], (D,), 0.5, 3.0, (), jnp.float32)
    shift_tangent = bell_draw(own_keys[5], (D,), 0.5, 3.0, (), jnp.float32)
    out_gate = jnp.clip(jax.random.uniform(own_keys[6], (D,), jnp.float32, 0.5, 2.0), 0.5, 2.0)
    out_gate_tangent = bell_draw(own_keys[7], (D,), 0.5, 3.0, (), jnp.float32)
    routes_keys = jax.random.split(jax.random.fold_in(own_keys[8], 1), TOKENS // TOK_DEV)
    routes_turns = jax.random.permutation(jax.random.fold_in(own_keys[8], 3), TOKENS // TOK_DEV)
    routes = jax.vmap(lambda own, number: shared_out(jax.random.fold_in(own_keys[8], 2), own, number, TOK_DEV, EXPERTS, 2, CAP, 2))(routes_keys, routes_turns).reshape((TOKENS, 2))
    router_gates = jnp.clip(0.05 + 0.9 * jax.random.uniform(own_keys[9], (TOKENS, 2), jnp.float32) ** levels(own_keys[9], (TOKENS, 2), ((0, 128),), -0.2, 0.2), 0.05, 0.95)
    router_tangents = bell_draw(own_keys[10], (TOKENS, 2), 0.5, 3.0, ((0, 128),), jnp.float32)
    gate_weight = bell_draw(keys[11], (EXPERTS, D, FF), D ** -0.5, 0.125, ((0, 16), (1, 8)))
    up_weight = bell_draw(keys[12], (EXPERTS, D, FF), D ** -0.5, 0.125, ((0, 16), (1, 8)))
    down_weight = bell_draw(keys[13], (EXPERTS, D, FF), FF ** -0.5, 0.25, ((0, 16), (1, 8)))
    return dict(tokens=tokens, token_tangent=token_tangent, mod_scale=mod_scale, mod_shift=mod_shift, scale_tangent=scale_tangent, shift_tangent=shift_tangent, out_gate=out_gate, out_gate_tangent=out_gate_tangent, routes=routes, router_gates=router_gates, router_tangents=router_tangents, gate_weight=gate_weight, up_weight=up_weight, down_weight=down_weight)


def modulate(tokens, token_tangent, mod_scale, mod_shift, scale_tangent, shift_tangent):
    primal = tokens.astype(jnp.float32)
    moving = token_tangent.astype(jnp.float32)
    inverse = lax.rsqrt(lax.optimization_barrier(jnp.mean(primal * primal, axis=-1, keepdims=True)) + 1e-06)
    normed = primal * inverse
    normed_tangent = (moving - normed * lax.optimization_barrier(jnp.mean(normed * moving, axis=-1, keepdims=True))) * inverse
    widened = 1.0 + mod_scale
    modded = (normed * widened + mod_shift).astype(jnp.bfloat16)
    modded_tangent = (normed_tangent * widened + normed * scale_tangent + shift_tangent).astype(jnp.bfloat16)
    return (modded, modded_tangent)

def expert_tangent(primal_rows, tangent_rows, gate_matrix, up_matrix, down_matrix):
    gate_sum = jnp.dot(primal_rows, gate_matrix, preferred_element_type=jnp.float32)
    gate_move = jnp.dot(tangent_rows, gate_matrix, preferred_element_type=jnp.float32)
    up_sum = jnp.dot(primal_rows, up_matrix, preferred_element_type=jnp.float32)
    up_move = jnp.dot(tangent_rows, up_matrix, preferred_element_type=jnp.float32)
    sigma = jax.nn.sigmoid(gate_sum)
    active = gate_sum * sigma
    slope = sigma * (1.0 + gate_sum * (1.0 - sigma))
    hidden = (active * up_sum).astype(jnp.bfloat16)
    hidden_tangent = (slope * gate_move * up_sum + active * up_move).astype(jnp.bfloat16)
    output = jnp.dot(hidden, down_matrix.T, preferred_element_type=jnp.float32).astype(jnp.bfloat16)
    output_tangent = jnp.dot(hidden_tangent, down_matrix.T, preferred_element_type=jnp.float32).astype(jnp.bfloat16)
    return (output, output_tangent)

def reference(tokens, token_tangent, mod_scale, mod_shift, scale_tangent, shift_tangent, out_gate, out_gate_tangent, routes, router_gates, router_tangents, gate_weight, up_weight, down_weight):
    modded, modded_tangent = modulate(tokens, token_tangent, mod_scale, mod_shift, scale_tangent, shift_tangent)
    assigned = TOKENS * 2
    longest = CAP * (TOKENS // TOK_DEV)
    flat_routes = routes.reshape(-1).astype(jnp.int32)

    def one_expert(index, carry):
        outputs, tangents = carry
        chosen = jnp.nonzero(flat_routes == index, size=longest, fill_value=assigned)[0].astype(jnp.int32)
        filled = chosen < assigned
        token_index = jnp.where(filled, chosen // 2, 0).astype(jnp.int32)
        primal_rows = jnp.where(filled[:, None], modded[token_index], jnp.zeros((), modded.dtype))
        tangent_rows = jnp.where(filled[:, None], modded_tangent[token_index], jnp.zeros((), modded.dtype))
        output, output_tangent = expert_tangent(primal_rows, tangent_rows, gate_weight[index], up_weight[index], down_weight[index])
        outputs = outputs.at[chosen].set(output, mode='drop')
        tangents = tangents.at[chosen].set(output_tangent, mode='drop')
        return (outputs, tangents)
    start = (jnp.zeros((assigned, D), modded.dtype), jnp.zeros((assigned, D), modded.dtype))
    outputs, tangents = lax.fori_loop(0, EXPERTS, one_expert, start)
    picked = outputs.astype(jnp.float32).reshape(TOKENS, 2, D)
    picked_tangent = tangents.astype(jnp.float32).reshape(TOKENS, 2, D)
    combined = lax.optimization_barrier(jnp.sum(router_gates[:, :, None] * picked, axis=1))
    combined_tangent = lax.optimization_barrier(jnp.sum(router_tangents[:, :, None] * picked + router_gates[:, :, None] * picked_tangent, axis=1))
    primal = tokens.astype(jnp.float32)
    moving = token_tangent.astype(jnp.float32)
    mixed = (primal + out_gate * combined).astype(jnp.bfloat16)
    mixed_tangent = (moving + out_gate_tangent * combined + out_gate * combined_tangent).astype(jnp.bfloat16)
    return (mixed, mixed_tangent)
```

```python
import jax
import jax.numpy as jnp
from jax import lax
from jax.experimental import pallas as pl
from jax.experimental.pallas import tpu as pltpu
from jax.sharding import PartitionSpec as P

MESH = pl.DeviceIdType.MESH
BF16, F32 = jnp.bfloat16, jnp.float32
NX, NY, NZ = 4, 4, 16
GROUP = 2 * NX
CAP = 32
CH = 64
HOP = 3
LEAD = 8


def mod(a, n):
    return lax.rem(a + 4 * n, n)


def moe_kernel(
    tokens, tangent, vectors, routes, gates, gate_moves, gate_w, up_w, down_w,
    mixed, mixed_tangent,
    own, weights, modded, picks, packed, rows, hidden, results, returned,
    own_sem, z_sem, y_sem, x_sem, back_sem,
    seed_core, seed_y, right_sem, left_sem, side_sem, packed_sem, results_sem,
):
    n_tokens, width = tokens.shape
    pieces = 2 * NY
    piece_rows = width // pieces
    rc = piece_rows // CH
    n_first = 8 * rc
    n_all = 12 * rc
    tile = 256
    half = width // 2
    x, k, z = lax.axis_index("dp"), lax.axis_index("ctx"), lax.axis_index("expert")
    y, c = k // 2, lax.rem(k, 2)
    me = 2 * x + c

    def place(j):
        return (j // 2, 2 * y + lax.rem(j, 2), z)

    def right_distance(j):
        return mod(z - j - 1, 8) + 1

    def expert(j, s):
        return mod(z - right_distance(j) + 8 * s, NZ)

    dr = right_distance(me)
    source = (lax.rem(z, 8) // 2) == x
    taker = lax.rem(z, 2)

    loads = [
        pltpu.make_async_copy(w, own.at[i], own_sem.at[i]) for i, w in enumerate((gate_w, up_w, down_w))
    ]
    for load in loads:
        load.start()

    barrier = pltpu.get_barrier_semaphore()
    peers = [(x, k, mod(z + 1, NZ)), (x, k, mod(z - 1, NZ))]
    for step in (1, -1):
        for core in range(2):
            peers.append((x, 2 * mod(y + step, NY) + core, z))
    for other in range(1, GROUP):
        peers.append(place(lax.rem(me + other, GROUP)))
    for peer in peers:
        pl.semaphore_signal(barrier, inc=1, device_id=peer, device_id_type=MESH)
    pl.semaphore_wait(barrier, len(peers))
    for load in loads:
        load.wait()

    def send(src, dst, send_sem, recv_sem, device):
        pltpu.make_async_remote_copy(
            src_ref=src, dst_ref=dst, send_sem=send_sem, recv_sem=recv_sem, device_id=device, device_id_type=MESH
        ).start()

    def wait(ref, sem):
        pltpu.make_async_copy(ref, ref, sem).wait()

    def decode(i):
        late = i >= n_first
        i = jnp.where(late, i - n_first, i)
        a = lax.rem(i, 2)
        n = i // 2
        r = lax.rem(n, rc)
        n = n // rc
        return jnp.where(late, 2, lax.rem(n, 2)), jnp.where(late, n, n // 2), r, a

    def seed(i):
        mat, p, r, a = decode(i)

        @pl.when(source & (i < n_all) & (p == c))
        def _():
            src = own.at[mat, r]
            dst = weights.at[1, mat, (2 * y + p) * rc + r]

            @pl.when((a == 0) & (c == taker))
            def _():
                pltpu.make_async_copy(src, dst, z_sem.at[1, i]).start()

            @pl.when((a == 0) & (c != taker))
            def _():
                send(src, dst, seed_core, z_sem.at[1, i], (x, 2 * y + taker, z))

            @pl.when(a == 1)
            def _():
                send(src, dst, seed_y, z_sem.at[1, i], (x, 2 * mod(y + 1, NY) + taker, z))

    def step(t, s):
        i = t - HOP * jnp.where(s == 0, dr, 8 - dr)

        @pl.when((i >= 0) & (i < n_all))
        def _():
            mat, p, r, a = decode(i)
            row = (2 * mod(y - a, NY) + p) * rc + r
            block = weights.at[s, mat, row]
            wait(block, z_sem.at[s, i])

            @pl.when(((s == 0) & (dr < 8)) | ((s == 1) & (dr == 8)))
            def _():
                send(block, weights.at[0, mat, row], right_sem, z_sem.at[0, i], (x, k, mod(z + 1, NZ)))

            @pl.when((s == 1) & (dr != 1))
            def _():
                send(block, weights.at[1, mat, row], left_sem, z_sem.at[1, i], (x, k, mod(z - 1, NZ)))

            side = jnp.where(a == 0, mod(y - 1, NY), mod(y + 1, NY))
            phase = jnp.where(mat < 2, 0, 1 + p)
            send(block, block, side_sem, y_sem.at[s, phase], (x, 2 * side + c, z))

    def first_products(s):
        wait(rows.at[s], x_sem.at[s])
        wait(weights.at[s, 0:2, 0 : 4 * rc], y_sem.at[s, 0])

        def column(n, _):
            cols = pl.ds(pl.multiple_of(n * tile, tile), tile)
            left = rows[s].reshape(GROUP * 2 * CAP, width)
            gate = jnp.dot(left, weights[s, 0, :, :, cols].reshape(width, tile), preferred_element_type=F32)
            up = jnp.dot(left, weights[s, 1, :, :, cols].reshape(width, tile), preferred_element_type=F32)
            gate, up = gate.reshape(GROUP, 2, CAP, tile), up.reshape(GROUP, 2, CAP, tile)
            u, du, v, dv = gate[:, 0], gate[:, 1], up[:, 0], up[:, 1]
            sigma = jax.nn.sigmoid(u)
            active = u * sigma
            slope = sigma * (1.0 + u * (1.0 - sigma))
            hidden[s, :, 0, :, cols] = (active * v).astype(BF16)
            hidden[s, :, 1, :, cols] = (slope * du * v + active * dv).astype(BF16)
            return 0

        lax.fori_loop(0, hidden.shape[-1] // tile, column, 0)

    def second_products(s, p):
        wait(weights.at[s, 2, 0 : 2 * rc], y_sem.at[s, 1 + p])

        def block(n, _):
            left = hidden[s].reshape(GROUP * 2 * CAP, hidden.shape[-1])
            right = weights[s, 2, pl.ds((2 * n + p) * rc, rc)].reshape(piece_rows, hidden.shape[-1])
            out = lax.dot_general(left, right, (((1,), (1,)), ((), ())), preferred_element_type=F32)
            cols = pl.ds(pl.multiple_of(n * piece_rows, piece_rows), piece_rows)
            results[s, p, :, :, :, cols] = out.astype(BF16).reshape(GROUP, 2, CAP, piece_rows)
            return 0

        lax.fori_loop(0, NY, block, 0)
        e = expert(me, s)
        pltpu.make_async_copy(results.at[s, p, me], returned.at[p, :, e], back_sem.at[p]).start()

        def give(other, _):
            j = lax.rem(me + other, GROUP)
            send(results.at[s, p, j], returned.at[p, :, e], results_sem, back_sem.at[p], place(j))
            return 0

        lax.fori_loop(1, GROUP, give, 0)

    def ahead(i, _):
        seed(i)
        return 0

    lax.fori_loop(0, LEAD, ahead, 0)

    lanes = lax.broadcasted_iota(jnp.int32, (n_tokens, 128), 1)
    named = [lanes == routes[:, i : i + 1] for i in range(2)]
    before = lax.broadcasted_iota(jnp.int32, (n_tokens, n_tokens), 0) > lax.broadcasted_iota(
        jnp.int32, (n_tokens, n_tokens), 1
    )
    counts = jnp.dot(
        before.astype(F32).astype(BF16),
        (named[0] | named[1]).astype(F32).astype(BF16),
        preferred_element_type=F32,
    )
    slots = lax.broadcasted_iota(jnp.int32, (n_tokens, NZ * CAP), 1)
    for i in range(2):
        position = jnp.sum(jnp.where(named[i], counts, 0.0), axis=1, keepdims=True).astype(jnp.int32)
        picks[i * n_tokens : (i + 1) * n_tokens] = (
            (slots == routes[:, i : i + 1] * CAP + position).astype(F32).astype(BF16)
        )

    def modulate(n, _):
        at = pl.ds(pl.multiple_of(n * 32, 32), 32)
        primal, moving = tokens[at].astype(F32), tangent[at].astype(F32)
        inverse = lax.rsqrt(jnp.mean(primal * primal, axis=-1, keepdims=True) + 1e-06)
        normed = primal * inverse
        normed_tangent = (moving - normed * jnp.mean(normed * moving, axis=-1, keepdims=True)) * inverse
        widened = 1.0 + vectors[0:1]
        modded[0, at] = (normed * widened + vectors[1:2]).astype(BF16)
        modded[1, at] = (normed_tangent * widened + normed * vectors[2:3] + vectors[3:4]).astype(BF16)
        return 0

    lax.fori_loop(0, n_tokens // 32, modulate, 0)

    def pack(n, _):
        cols = pl.ds(pl.multiple_of(n * tile, tile), tile)
        chosen = picks[0:n_tokens] + picks[n_tokens : 2 * n_tokens]
        for i in range(2):
            out = lax.dot_general(
                chosen, modded[i, :, cols], (((0,), (0,)), ((), ())), preferred_element_type=F32
            )
            packed[:, i, :, cols] = out.astype(BF16).reshape(NZ, CAP, tile)
        return 0

    lax.fori_loop(0, width // tile, pack, 0)

    def deal(n, _):
        other = lax.rem(n, GROUP)
        j = lax.rem(me + other, GROUP)
        near = jnp.where(right_distance(j) <= 4, 0, 1)
        s = jnp.where(n < GROUP, near, 1 - near)
        e = expert(j, s)

        @pl.when(other == 0)
        def _():
            pltpu.make_async_copy(packed.at[e], rows.at[s, me], x_sem.at[s]).start()

        @pl.when(other != 0)
        def _():
            send(packed.at[e], rows.at[s, me], packed_sem, x_sem.at[s], place(j))

        return 0

    lax.fori_loop(0, 2 * GROUP, deal, 0)

    def turn(t, _):
        seed(t + LEAD)

        def stream(s, _):
            step(t, s)
            passed = t - HOP * jnp.where(s == 0, dr, 8 - dr) - HOP

            @pl.when(passed == n_first)
            def _():
                first_products(s)

            @pl.when((passed == n_first + 2 * rc) | (passed == n_all))
            def _():
                second_products(s, jnp.where(passed == n_all, 1, 0))

            return 0

        lax.fori_loop(0, 2, stream, 0)
        return 0

    lax.fori_loop(0, n_all + 9 * HOP + 1, turn, 0)

    for p in range(2):
        wait(returned.at[p], back_sem.at[p])

        def combine(n, _, p=p):
            cols = pl.ds(pl.multiple_of(n * piece_rows, piece_rows), piece_rows)
            to = pl.ds(pl.multiple_of((2 * n + p) * piece_rows, piece_rows), piece_rows)
            out, out_tangent = [
                jnp.dot(
                    picks[...],
                    returned[p, i, :, :, cols].reshape(NZ * CAP, piece_rows),
                    preferred_element_type=F32,
                )
                for i in range(2)
            ]
            g0, g1 = gates[:, 0:1], gates[:, 1:2]
            y0, y1 = out[:n_tokens], out[n_tokens:]
            total = g0 * y0 + g1 * y1
            moved = (gate_moves[:, 0:1] * y0 + g0 * out_tangent[:n_tokens]) + (
                gate_moves[:, 1:2] * y1 + g1 * out_tangent[n_tokens:]
            )
            opened, opened_move = vectors[4:5, to], vectors[5:6, to]
            mixed[:, to] = (tokens[:, to].astype(F32) + opened * total).astype(BF16)
            mixed_tangent[:, to] = (
                tangent[:, to].astype(F32) + opened_move * total + opened * moved
            ).astype(BF16)
            return 0

        lax.fori_loop(0, half // piece_rows, combine, 0)

    wait(packed.at[0 : 2 * (GROUP - 1)], packed_sem)
    wait(results.at[:, :, 0 : GROUP - 1], results_sem)
    wait(weights.at[0, :, 0 : 4 * rc], right_sem)
    wait(weights.at[:, :, 0 : 4 * rc], side_sem)

    @pl.when(dr != 1)
    def _():
        wait(weights.at[1, :, 0 : 4 * rc], left_sem)

    @pl.when(source)
    def _():
        wait(own, seed_y)

    @pl.when(source & (c != taker))
    def _():
        wait(own, seed_core)


def body(
    tokens,
    token_tangent,
    mod_scale,
    mod_shift,
    scale_tangent,
    shift_tangent,
    out_gate,
    out_gate_tangent,
    routes,
    router_gates,
    router_tangents,
    gate_weight,
    up_weight,
    down_weight,
):
    n_tokens, width = tokens.shape
    _, piece_rows, inner = gate_weight.shape
    rc = piece_rows // CH
    vectors = jnp.stack(
        [mod_scale, mod_shift, scale_tangent, shift_tangent, out_gate, out_gate_tangent, out_gate, out_gate]
    )
    shape = (rc, CH, inner)
    vmem, anywhere = pl.BlockSpec(memory_space=pltpu.VMEM), pl.BlockSpec(memory_space=pl.ANY)
    dma = pltpu.SemaphoreType.DMA
    slab = (2, CAP, width)
    return tuple(pl.pallas_call(
        moe_kernel,
        name="moe",
        out_shape=[jax.ShapeDtypeStruct(tokens.shape, BF16)] * 2,
        in_specs=[vmem] * 6 + [anywhere] * 3,
        out_specs=[vmem] * 2,
        scratch_shapes=[
            pltpu.VMEM((3, *shape), BF16),
            pltpu.VMEM((2, 3, 2 * NY * rc, CH, inner), BF16),
            pltpu.VMEM((2, n_tokens, width), BF16),
            pltpu.VMEM((2 * n_tokens, NZ * CAP), BF16),
            pltpu.VMEM((NZ, *slab), BF16),
            pltpu.VMEM((2, GROUP, *slab), BF16),
            pltpu.VMEM((2, GROUP, 2, CAP, inner), BF16),
            pltpu.VMEM((2, 2, GROUP, 2, CAP, width // 2), BF16),
            pltpu.VMEM((2, 2, NZ, CAP, width // 2), BF16),
            dma((3,)),
            dma((2, 12 * rc)),
            dma((2, 3)),
            dma((2,)),
            dma((2,)),
        ]
        + [dma] * 7,
        compiler_params=pltpu.CompilerParams(
            collective_id=0, has_side_effects=True, vmem_limit_bytes=60 * 2**20
        ),
    )(
        tokens,
        token_tangent,
        vectors,
        routes,
        router_gates,
        router_tangents,
        gate_weight.reshape(shape),
        up_weight.reshape(shape),
        down_weight.reshape(shape),
    ))


def solution(mesh):
    rows = P(("dp", "ctx", "expert"), None)
    expert_rows = P("expert", "ctx", None)
    in_specs = (rows,) * 2 + (P("dp"),) * 6 + (rows,) * 3 + (expert_rows,) * 3
    return jax.shard_map(body, mesh=mesh, in_specs=in_specs, out_specs=(rows, rows), check_vma=False)
```

```python
import jax
import jax.numpy as jnp
from jax import lax
from jax.experimental import pallas as pl
from jax.experimental.pallas import tpu as pltpu
from jax.sharding import PartitionSpec as P

MESH = pl.DeviceIdType.MESH
BF16, F32 = jnp.bfloat16, jnp.float32
NX, NY, NZ = 4, 4, 16
GROUP = 2 * NX
CAP = 32
CH = 32
JOIN = 4
HOP = 6
SIDE = 3
LEAD = 8
PARTS = 4


def mod(a, n):
    return lax.rem(a + 4 * n, n)


def moe_kernel(
    tokens, tangent, scale, shift, scale_move, shift_move, opened, opened_move,
    routes, gates, gate_moves, gate_w, up_w, down_w,
    mixed, mixed_tangent,
    own, weights, modded, slots, picks, spread, packed, rows, hidden, results, returned,
    own_sem, z_sem, y_sem, x_sem, back_sem,
    seed_core, seed_y, right_sem, left_sem, side_sem, packed_sem, results_sem,
):
    n_tokens, width = tokens.shape
    pieces = 2 * NY
    piece_rows = width // pieces
    rc = piece_rows // CH
    n_first = 4 * rc
    n_all = 6 * rc
    span = width // PARTS
    strip = span // NY
    tile = 256
    x, k, z = lax.axis_index("dp"), lax.axis_index("ctx"), lax.axis_index("expert")
    y, c = k >> 1, k & 1
    me = 2 * x + c

    def place(j):
        return (j >> 1, 2 * y + (j & 1), z)

    def right_distance(j):
        return mod(z - j - 1, 8) + 1

    def expert(j, s):
        return mod(z - right_distance(j) + 8 * s, NZ)

    dr = right_distance(me)
    source = ((z & 7) >> 1) == x
    taker = z & 1

    loads = [
        pltpu.make_async_copy(w, own.at[i], own_sem.at[i]) for i, w in enumerate((gate_w, up_w, down_w))
    ]
    for load in loads:
        load.start()

    barrier = pltpu.get_barrier_semaphore()
    peers = [(x, k, mod(z + 1, NZ)), (x, k, mod(z - 1, NZ))]
    for step in (1, -1):
        for core in range(2):
            peers.append((x, 2 * mod(y + step, NY) + core, z))
    for other in range(1, GROUP):
        peers.append(place(lax.rem(me + other, GROUP)))
    for peer in peers:
        pl.semaphore_signal(barrier, inc=1, device_id=peer, device_id_type=MESH)

    pl.semaphore_wait(barrier, len(peers))
    for load in loads:
        load.wait()

    def send(src, dst, send_sem, recv_sem, device):
        pltpu.make_async_remote_copy(
            src_ref=src, dst_ref=dst, send_sem=send_sem, recv_sem=recv_sem, device_id=device, device_id_type=MESH
        ).start()

    def wait(ref, sem):
        pltpu.make_async_copy(ref, ref, sem).wait()

    ahead, behind = mod(y + 1, NY), mod(y - 1, NY)
    lag = ((HOP * dr) >> 1, (HOP * (8 - dr)) >> 1)

    def decode(j):
        n, r = lax.div(j, rc), lax.rem(j, rc)
        return n >> 1, n & 1, r, (lax.div(r, JOIN) & 1) == 1

    def seed(j):
        mat, p, r, turned = decode(j)

        @pl.when(source & (j < n_all) & (p == c))
        def _():
            src = own.at[mat, r]
            dst = weights.at[1, (8 * mat + 2 * y + p) * rc + r]

            @pl.when(c == taker)
            def _():
                pltpu.make_async_copy(src, dst, z_sem.at[1, 2 * j]).start()

            @pl.when(c != taker)
            def _():
                send(src, dst, seed_core, z_sem.at[1, 2 * j], (x, 2 * y + taker, z))

            column = jnp.where(turned, behind, ahead)
            send(src, dst, seed_y, z_sem.at[1, 2 * j + 1], (x, 2 * column + taker, z))

    def step(t, s):
        j = t - lag[s]

        @pl.when((j >= 0) & (j < n_all))
        def _():
            mat, p, r, turned = decode(j)
            base = (8 * mat + p) * rc + r
            second = jnp.where(turned, ahead, behind)
            for a, column in enumerate((y, second)):
                row = base + 2 * rc * column
                block = weights.at[s, row]
                i = 2 * j + a
                wait(block, z_sem.at[s, i])

                @pl.when(dr < 8 if s == 0 else dr == 8)
                def _():
                    send(block, weights.at[0, row], right_sem, z_sem.at[0, i], (x, k, mod(z + 1, NZ)))

                if s == 1:

                    @pl.when(dr != 1)
                    def _():
                        send(block, weights.at[1, row], left_sem, z_sem.at[1, i], (x, k, mod(z - 1, NZ)))

            @pl.when(lax.rem(r, JOIN) == JOIN - 1)
            def _():
                part = jnp.where(mat < 2, 0, 1 + lax.div(j - n_first, 2 * rc // PARTS))
                for a, column in enumerate((y, second)):
                    joined = weights.at[s, pl.ds(base + 2 * rc * column - (JOIN - 1), JOIN)]
                    side = jnp.where(turned, behind, ahead) if a else second
                    send(joined, joined, side_sem, y_sem.at[s, part], (x, 2 * side + c, z))

    def first_products(s, n):
        @pl.when(n == 0)
        def _():
            wait(rows.at[s], x_sem.at[s])
            wait(weights.at[s, 0 : 8 * rc], y_sem.at[s, 0])

        few = tile // 2
        cols = pl.ds(pl.multiple_of(n * few, few), few)
        left = rows[s].reshape(GROUP * 2 * CAP, width)
        right = jnp.concatenate(
            [weights[s, i * 8 * rc : (i + 1) * 8 * rc, :, cols].reshape(width, few) for i in range(2)], axis=1
        )
        out = jnp.dot(left, right, preferred_element_type=F32).reshape(GROUP, 2, CAP, tile)
        u, du, v, dv = out[:, 0, :, :few], out[:, 1, :, :few], out[:, 0, :, few:], out[:, 1, :, few:]
        sigma = jax.nn.sigmoid(u)
        active = u * sigma
        slope = sigma * (1.0 + u * (1.0 - sigma))
        hidden[s, :, 0, :, cols] = (active * v).astype(BF16)
        hidden[s, :, 1, :, cols] = (slope * du * v + active * dv).astype(BF16)

    def second_products(s, f):
        wait(weights.at[s, 0 : 4 * rc // PARTS], y_sem.at[s, 1 + f])
        few = strip // CH
        start = (16 + lax.div(f, PARTS // 2)) * rc + lax.rem(f, PARTS // 2) * few
        left = hidden[s].reshape(GROUP * 2 * CAP, hidden.shape[-1])
        for n in range(span // tile):
            right = jnp.concatenate(
                [
                    weights[s, pl.ds(start + 2 * rc * i, few)].reshape(strip, hidden.shape[-1])
                    for i in range(n * tile // strip, (n + 1) * tile // strip)
                ],
                axis=0,
            )
            out = lax.dot_general(left, right, (((1,), (1,)), ((), ())), preferred_element_type=F32)
            results[s, f, :, :, :, n * tile : (n + 1) * tile] = out.astype(BF16).reshape(GROUP, 2, CAP, tile)

    def give(s, f, first):
        e = expert(me, s)

        @pl.when(first == 0)
        def _():
            pltpu.make_async_copy(results.at[s, f, me], returned.at[f, :, e], back_sem.at[f]).start()

        def one(other, _):
            j = (me + other) & (GROUP - 1)
            send(results.at[s, f, j], returned.at[f, :, e], results_sem, back_sem.at[f], place(j))
            return 0

        lax.fori_loop(jnp.maximum(first, 1), first + GROUP // 2, one, 0)

    def go_ahead(j, _):
        seed(j)
        return 0

    lax.fori_loop(0, LEAD, go_ahead, 0)

    def choose(i):
        sublanes = lax.broadcasted_iota(jnp.int32, (NZ, n_tokens), 0)
        named = [sublanes == routes[j : j + 1] for j in range(2)]
        before = lax.broadcasted_iota(jnp.int32, (n_tokens, n_tokens), 0) < lax.broadcasted_iota(
            jnp.int32, (n_tokens, n_tokens), 1
        )
        counts = jnp.dot(
            (named[0] | named[1]).astype(F32).astype(BF16),
            before.astype(F32).astype(BF16),
            preferred_element_type=F32,
        )
        places = lax.broadcasted_iota(jnp.int32, (NZ * CAP, n_tokens), 0)
        position = jnp.sum(jnp.where(named[i], counts, 0.0), axis=0, keepdims=True).astype(jnp.int32)
        taken = (places == routes[i : i + 1] * CAP + position).astype(F32)
        picks[i * n_tokens : (i + 1) * n_tokens] = taken.T.astype(BF16)
        slots[...] = taken.astype(BF16) if i == 0 else slots[...] + taken.astype(BF16)
        weight = (gates, gate_moves)[i]
        for j in range(2):
            spread[2 * i + j] = jnp.broadcast_to(weight[j : j + 1], (n_tokens, n_tokens)).T

    def modulate(n):
        at = pl.ds(pl.multiple_of(n * 32, 32), 32)
        primal, moving = tokens[at].astype(F32), tangent[at].astype(F32)
        inverse = lax.rsqrt(jnp.mean(primal * primal, axis=-1, keepdims=True) + 1e-06)
        normed = primal * inverse
        normed_tangent = (moving - normed * jnp.mean(normed * moving, axis=-1, keepdims=True)) * inverse
        widened = 1.0 + scale[...]
        modded[0, at] = (normed * widened + shift[...]).astype(BF16)
        modded[1, at] = (normed_tangent * widened + normed * scale_move[...] + shift_move[...]).astype(BF16)

    def pack(n):
        cols = pl.ds(pl.multiple_of(n * 2 * tile, 2 * tile), 2 * tile)
        for i in range(2):
            out = jnp.dot(slots[...], modded[i, :, cols], preferred_element_type=F32)
            packed[:, i, :, cols] = out.astype(BF16).reshape(NZ, CAP, 2 * tile)

    def deal(n, _):
        other = lax.rem(n, GROUP)
        j = lax.rem(me + other, GROUP)
        near = jnp.where(right_distance(j) <= 4, 0, 1)
        s = jnp.where(n < GROUP, near, 1 - near)
        e = expert(j, s)

        @pl.when(other == 0)
        def _():
            pltpu.make_async_copy(packed.at[e], rows.at[s, me], x_sem.at[s]).start()

        @pl.when(other != 0)
        def _():
            send(packed.at[e], rows.at[s, me], packed_sem, x_sem.at[s], place(j))

        return 0


    n_mods, n_packs = n_tokens // 32, width // (2 * tile)

    def turn(t, _):
        seed(t + LEAD)
        step(t, 0)
        step(t, 1)

        for i in range(2):

            @pl.when(t == i)
            def _(i=i):
                choose(i)

        @pl.when((t >= 2) & (t < 2 + n_mods))
        def _():
            modulate(t - 2)

        @pl.when((t >= 2 + n_mods) & (t < 2 + n_mods + n_packs))
        def _():
            pack(t - 2 - n_mods)

        dealt = t - 2 - n_mods - n_packs

        @pl.when((dealt >= 0) & (dealt < 4))
        def _():
            lax.fori_loop(dealt * GROUP // 2, (dealt + 1) * GROUP // 2, deal, 0)

        def stream(s, _):
            u = t - jnp.where(s == 0, lag[0], lag[1]) - SIDE - n_first
            n_cols = 2 * hidden.shape[-1] // tile

            @pl.when((u >= 0) & (u < n_cols))
            def _():
                first_products(s, u)

            part_steps = 2 * rc // PARTS
            f = lax.div(u, part_steps) - 1
            at = lax.rem(u, part_steps)

            @pl.when((f >= 0) & (f < PARTS))
            def _():
                @pl.when(at == 0)
                def _():
                    second_products(s, f)

                @pl.when((at == 1) | (at == 2))
                def _():
                    give(s, f, (at - 1) * (GROUP // 2))

            return 0

        lax.fori_loop(0, 2, stream, 0)
        return 0

    lax.fori_loop(0, n_all + 4 * HOP + SIDE + 3, turn, 0)

    for f in range(PARTS):
        wait(returned.at[f], back_sem.at[f])
        for n in range(span // tile):
            out, out_tangent = [
                jnp.dot(
                    picks[...],
                    returned[f, i, :, :, n * tile : (n + 1) * tile].reshape(NZ * CAP, tile),
                    preferred_element_type=F32,
                )
                for i in range(2)
            ]
            for i in range(tile // strip):
                at = (2 * (n * tile // strip + i) + f // (PARTS // 2)) * piece_rows + f % (PARTS // 2) * strip
                to, of = slice(at, at + strip), slice(i * strip, (i + 1) * strip)
                g0, g1, m0, m1 = [
                    jnp.concatenate([spread[j]] * (strip // n_tokens), axis=1) if strip > n_tokens else spread[j]
                    for j in range(4)
                ]
                y0, y1 = out[:n_tokens, of], out[n_tokens:, of]
                total = g0 * y0 + g1 * y1
                moved = (m0 * y0 + g0 * out_tangent[:n_tokens, of]) + (m1 * y1 + g1 * out_tangent[n_tokens:, of])
                mixed[:, to] = (tokens[:, to].astype(F32) + opened[:, to] * total).astype(BF16)
                mixed_tangent[:, to] = (
                    tangent[:, to].astype(F32) + opened_move[:, to] * total + opened[:, to] * moved
                ).astype(BF16)

    wait(packed.at[0 : 2 * (GROUP - 1)], packed_sem)
    wait(results.at[:, :, 0 : GROUP - 1], results_sem)
    wait(weights.at[0, 0 : 12 * rc], right_sem)
    wait(weights.at[:, 0 : 12 * rc], side_sem)

    @pl.when(dr != 1)
    def _():
        wait(weights.at[1, 0 : 12 * rc], left_sem)

    @pl.when(source)
    def _():
        wait(own, seed_y)

    @pl.when(source & (c != taker))
    def _():
        wait(own, seed_core)


def body(
    tokens,
    token_tangent,
    mod_scale,
    mod_shift,
    scale_tangent,
    shift_tangent,
    out_gate,
    out_gate_tangent,
    routes,
    router_gates,
    router_tangents,
    gate_weight,
    up_weight,
    down_weight,
):
    n_tokens, width = tokens.shape
    _, piece_rows, inner = gate_weight.shape
    rc = piece_rows // CH
    shape = (rc, CH, inner)
    vmem, anywhere = pl.BlockSpec(memory_space=pltpu.VMEM), pl.BlockSpec(memory_space=pl.ANY)
    dma = pltpu.SemaphoreType.DMA
    slab = (2, CAP, width)
    return tuple(pl.pallas_call(
        moe_kernel,
        name="moe",
        out_shape=[jax.ShapeDtypeStruct(tokens.shape, BF16)] * 2,
        in_specs=[vmem] * 11 + [anywhere] * 3,
        out_specs=[vmem] * 2,
        scratch_shapes=[
            pltpu.VMEM((3, *shape), BF16),
            pltpu.VMEM((2, 3 * 2 * NY * rc, CH, inner), BF16),
            pltpu.VMEM((2, n_tokens, width), BF16),
            pltpu.VMEM((NZ * CAP, n_tokens), BF16),
            pltpu.VMEM((2 * n_tokens, NZ * CAP), BF16),
            pltpu.VMEM((4, n_tokens, n_tokens), F32),
            pltpu.VMEM((NZ, *slab), BF16),
            pltpu.VMEM((2, GROUP, *slab), BF16),
            pltpu.VMEM((2, GROUP, 2, CAP, inner), BF16),
            pltpu.VMEM((2, PARTS, GROUP, 2, CAP, width // PARTS), BF16),
            pltpu.VMEM((PARTS, 2, NZ, CAP, width // PARTS), BF16),
            dma((3,)),
            dma((2, 12 * rc)),
            dma((2, 1 + PARTS)),
            dma((2,)),
            dma((PARTS,)),
        ]
        + [dma] * 7,
        compiler_params=pltpu.CompilerParams(
            collective_id=0, has_side_effects=True, vmem_limit_bytes=60 * 2**20
        ),
    )(
        tokens,
        token_tangent,
        *[
            v.reshape(1, width)
            for v in (mod_scale, mod_shift, scale_tangent, shift_tangent, out_gate, out_gate_tangent)
        ],
        routes.T,
        router_gates.T,
        router_tangents.T,
        gate_weight.reshape(shape),
        up_weight.reshape(shape),
        down_weight.reshape(shape),
    ))


def solution(mesh):
    rows = P(("dp", "ctx", "expert"), None)
    expert_rows = P("expert", "ctx", None)
    in_specs = (rows,) * 2 + (P("dp"),) * 6 + (rows,) * 3 + (expert_rows,) * 3
    return jax.shard_map(body, mesh=mesh, in_specs=in_specs, out_specs=(rows, rows), check_vma=False)
```

```python
import jax
import jax.numpy as jnp
from jax import lax
from jax.experimental import pallas as pl
from jax.experimental.pallas import tpu as pltpu
from jax.sharding import PartitionSpec as P

MESH = pl.DeviceIdType.MESH
BF16, F32 = jnp.bfloat16, jnp.float32
NX, NY, NZ = 4, 4, 16
GROUP = 2 * NX
CAP = 32
CH = 32
JOIN = 2
HOP = 6
SIDE = 3
DEAL = 4
LEAD = 8
PARTS = 4


def mod(a, n):
    return lax.rem(a + 4 * n, n)


def moe_kernel(
    tokens_in, tangent_in, scale, shift, scale_move, shift_move, opened, opened_move,
    routes, gates, gate_moves, gate_w, up_w, down_w,
    mixed_out, mixed_tangent_out,
    tokens, tangent, mixed, mixed_tangent, row_sem, out_sem,
    own, weights, modded, slots, picks, spread, packed, rows, hidden, results, returned,
    own_sem, z_sem, y_sem, x_sem, back_sem,
    seed_core, seed_y, right_sem, left_sem, side_sem, packed_sem, results_sem,
):
    n_tokens, width = tokens.shape
    pieces = 2 * NY
    piece_rows = width // pieces
    rc = piece_rows // CH
    n_first = 4 * rc
    n_all = 6 * rc
    span = width // PARTS
    strip = span // NY
    tile = 256
    x, k, z = lax.axis_index("dp"), lax.axis_index("ctx"), lax.axis_index("expert")
    y, c = k >> 1, k & 1
    me = 2 * x + c

    def place(j):
        return (j >> 1, 2 * y + (j & 1), z)

    def right_distance(j):
        return mod(z - j - 1, 8) + 1

    def expert(j, s):
        return mod(z - right_distance(j) + 8 * s, NZ)

    dr = right_distance(me)
    source = ((z & 7) >> 1) == x
    taker = z & 1

    loads = [
        pltpu.make_async_copy(w, own.at[i], own_sem.at[i]) for i, w in enumerate((gate_w, up_w, down_w))
    ]
    loads += [
        pltpu.make_async_copy(a, b, row_sem.at[i])
        for i, (a, b) in enumerate(((tokens_in, tokens), (tangent_in, tangent)))
    ]
    for load in loads:
        load.start()

    barrier = pltpu.get_barrier_semaphore()
    peers = [(x, k, mod(z + 1, NZ)), (x, k, mod(z - 1, NZ))]
    for step in (1, -1):
        for core in range(2):
            peers.append((x, 2 * mod(y + step, NY) + core, z))
    for other in range(1, GROUP):
        peers.append(place(lax.rem(me + other, GROUP)))
    for peer in peers:
        pl.semaphore_signal(barrier, inc=1, device_id=peer, device_id_type=MESH)

    pl.semaphore_wait(barrier, len(peers))
    for load in loads[:3]:
        load.wait()

    def send(src, dst, send_sem, recv_sem, device):
        pltpu.make_async_remote_copy(
            src_ref=src, dst_ref=dst, send_sem=send_sem, recv_sem=recv_sem, device_id=device, device_id_type=MESH
        ).start()

    def wait(ref, sem):
        pltpu.make_async_copy(ref, ref, sem).wait()

    ahead, behind = mod(y + 1, NY), mod(y - 1, NY)
    lag = ((HOP * dr) >> 1, (HOP * (8 - dr)) >> 1)

    def decode(j):
        n, r = lax.div(j, rc), lax.rem(j, rc)
        return n >> 1, n & 1, r, (lax.div(r, JOIN) & 1) == 1

    def seed(j):
        mat, p, r, turned = decode(j)

        @pl.when(source & (j < n_all) & (p == c))
        def _():
            src = own.at[mat, r]
            dst = weights.at[1, (8 * mat + 2 * y + p) * rc + r]

            @pl.when(c == taker)
            def _():
                pltpu.make_async_copy(src, dst, z_sem.at[1, 2 * j]).start()

            @pl.when(c != taker)
            def _():
                send(src, dst, seed_core, z_sem.at[1, 2 * j], (x, 2 * y + taker, z))

            column = jnp.where(turned, behind, ahead)
            send(src, dst, seed_y, z_sem.at[1, 2 * j + 1], (x, 2 * column + taker, z))

    def step(t, s):
        j = t - lag[s]

        @pl.when((j >= 0) & (j < n_all))
        def _():
            mat, p, r, turned = decode(j)
            base = (8 * mat + p) * rc + r
            second = jnp.where(turned, ahead, behind)
            for a, column in enumerate((y, second)):
                row = base + 2 * rc * column
                block = weights.at[s, row]
                i = 2 * j + a
                wait(block, z_sem.at[s, i])

                @pl.when(dr < 8 if s == 0 else dr == 8)
                def _():
                    send(block, weights.at[0, row], right_sem, z_sem.at[0, i], (x, k, mod(z + 1, NZ)))

                if s == 1:

                    @pl.when(dr != 1)
                    def _():
                        send(block, weights.at[1, row], left_sem, z_sem.at[1, i], (x, k, mod(z - 1, NZ)))

            @pl.when(lax.rem(r, JOIN) == JOIN - 1)
            def _():
                part = jnp.where(mat < 2, 0, 1 + lax.div(j - n_first, 2 * rc // PARTS))
                for a, column in enumerate((y, second)):
                    joined = weights.at[s, pl.ds(base + 2 * rc * column - (JOIN - 1), JOIN)]
                    side = jnp.where(turned, behind, ahead) if a else second
                    send(joined, joined, side_sem, y_sem.at[s, part], (x, 2 * side + c, z))

    def first_products(s, n):
        @pl.when(n == 0)
        def _():
            wait(rows.at[s], x_sem.at[s])
            wait(weights.at[s, 0 : 8 * rc], y_sem.at[s, 0])

        few = tile // 2
        cols = pl.ds(pl.multiple_of(n * few, few), few)
        left = rows[s].reshape(GROUP * 2 * CAP, width)
        right = jnp.concatenate(
            [weights[s, i * 8 * rc : (i + 1) * 8 * rc, :, cols].reshape(width, few) for i in range(2)], axis=1
        )
        out = jnp.dot(left, right, preferred_element_type=F32).reshape(GROUP, 2, CAP, tile)
        u, du, v, dv = out[:, 0, :, :few], out[:, 1, :, :few], out[:, 0, :, few:], out[:, 1, :, few:]
        sigma = jax.nn.sigmoid(u)
        active = u * sigma
        slope = sigma * (1.0 + u * (1.0 - sigma))
        hidden[s, :, 0, :, cols] = (active * v).astype(BF16)
        hidden[s, :, 1, :, cols] = (slope * du * v + active * dv).astype(BF16)

    def second_products(s, f):
        wait(weights.at[s, 0 : 4 * rc // PARTS], y_sem.at[s, 1 + f])
        few = strip // CH
        start = (16 + lax.div(f, PARTS // 2)) * rc + lax.rem(f, PARTS // 2) * few
        left = hidden[s].reshape(GROUP * 2 * CAP, hidden.shape[-1])
        for n in range(span // tile):
            right = jnp.concatenate(
                [
                    weights[s, pl.ds(start + 2 * rc * i, few)].reshape(strip, hidden.shape[-1])
                    for i in range(n * tile // strip, (n + 1) * tile // strip)
                ],
                axis=0,
            )
            out = lax.dot_general(left, right, (((1,), (1,)), ((), ())), preferred_element_type=F32)
            results[s, f, :, :, :, n * tile : (n + 1) * tile] = out.astype(BF16).reshape(GROUP, 2, CAP, tile)

    def give(s, f, first):
        e = expert(me, s)

        @pl.when(first == 0)
        def _():
            pltpu.make_async_copy(results.at[s, f, me], returned.at[f, :, e], back_sem.at[f]).start()

        def one(other, _):
            j = (me + other) & (GROUP - 1)
            send(results.at[s, f, j], returned.at[f, :, e], results_sem, back_sem.at[f], place(j))
            return 0

        lax.fori_loop(jnp.maximum(first, 1), first + GROUP // 2, one, 0)

    def go_ahead(j, _):
        seed(j)
        return 0

    lax.fori_loop(0, LEAD, go_ahead, 0)

    def choose(i):
        sublanes = lax.broadcasted_iota(jnp.int32, (NZ, n_tokens), 0)
        named = [sublanes == routes[j : j + 1] for j in range(2)]
        before = lax.broadcasted_iota(jnp.int32, (n_tokens, n_tokens), 0) < lax.broadcasted_iota(
            jnp.int32, (n_tokens, n_tokens), 1
        )
        counts = jnp.dot(
            (named[0] | named[1]).astype(F32).astype(BF16),
            before.astype(F32).astype(BF16),
            preferred_element_type=F32,
        )
        places = lax.broadcasted_iota(jnp.int32, (NZ * CAP, n_tokens), 0)
        position = jnp.sum(jnp.where(named[i], counts, 0.0), axis=0, keepdims=True).astype(jnp.int32)
        taken = (places == routes[i : i + 1] * CAP + position).astype(F32)
        picks[i * n_tokens : (i + 1) * n_tokens] = taken.T.astype(BF16)
        slots[...] = taken.astype(BF16) if i == 0 else slots[...] + taken.astype(BF16)
        weight = (gates, gate_moves)[i]
        for j in range(2):
            spread[2 * i + j] = jnp.broadcast_to(weight[j : j + 1], (n_tokens, n_tokens)).T

    def modulate(n):
        at = pl.ds(pl.multiple_of(n * 32, 32), 32)
        primal, moving = tokens[at].astype(F32), tangent[at].astype(F32)
        inverse = lax.rsqrt(jnp.mean(primal * primal, axis=-1, keepdims=True) + 1e-06)
        normed = primal * inverse
        normed_tangent = (moving - normed * jnp.mean(normed * moving, axis=-1, keepdims=True)) * inverse
        widened = 1.0 + scale[...]
        modded[0, at] = (normed * widened + shift[...]).astype(BF16)
        modded[1, at] = (normed_tangent * widened + normed * scale_move[...] + shift_move[...]).astype(BF16)

    def deal(g):
        dealt = []
        for i in range(DEAL):
            n = DEAL * g + i
            j = (me + n) & (GROUP - 1)
            near = jnp.where(right_distance(j) <= 4, 0, 1)
            s = jnp.where(n < GROUP, near, 1 - near)
            dealt.append((n, j, s, expert(j, s)))
        chosen = jnp.concatenate(
            [slots[pl.ds(pl.multiple_of(e * CAP, CAP), CAP)] for _, _, _, e in dealt], axis=0
        )
        for at in range(0, width, 2 * tile):
            cols = slice(at, at + 2 * tile)
            for i in range(2):
                out = jnp.dot(chosen, modded[i, :, cols], preferred_element_type=F32)
                packed[pl.ds(DEAL * g, DEAL), i, :, cols] = out.astype(BF16).reshape(DEAL, CAP, 2 * tile)
        for i, (n, j, s, _) in enumerate(dealt):
            if i == 0:

                @pl.when(j == me)
                def _(n=n, s=s):
                    pltpu.make_async_copy(packed.at[n], rows.at[s, me], x_sem.at[s]).start()

                @pl.when(j != me)
                def _(n=n, s=s, j=j):
                    send(packed.at[n], rows.at[s, me], packed_sem, x_sem.at[s], place(j))

            else:
                send(packed.at[n], rows.at[s, me], packed_sem, x_sem.at[s], place(j))

    def turn(t, _):
        seed(t + LEAD)
        step(t, 0)
        step(t, 1)

        for i in range(2):

            @pl.when(t == i)
            def _(i=i):
                choose(i)
                loads[3 + i].wait()

        @pl.when((t >= 2) & (t < 4))
        def _():
            modulate(2 * t - 4)
            modulate(2 * t - 3)

        @pl.when((t >= 4) & (t < 4 + 2 * GROUP // DEAL))
        def _():
            deal(t - 4)

        def stream(s, _):
            u = t - jnp.where(s == 0, lag[0], lag[1]) - SIDE - n_first
            n_cols = 2 * hidden.shape[-1] // tile

            @pl.when((u >= 0) & (u < n_cols))
            def _():
                first_products(s, u)

            part_steps = 2 * rc // PARTS
            f = lax.div(u, part_steps) - 1
            at = lax.rem(u, part_steps)

            @pl.when((f >= 0) & (f < PARTS))
            def _():
                @pl.when(at == 0)
                def _():
                    second_products(s, f)

                @pl.when((at == 1) | (at == 2))
                def _():
                    give(s, f, (at - 1) * (GROUP // 2))

            return 0

        lax.fori_loop(0, 2, stream, 0)
        return 0

    lax.fori_loop(0, n_all + 4 * HOP + SIDE + 3, turn, 0)

    outs = []
    for f in range(PARTS):
        wait(returned.at[f], back_sem.at[f])
        for n in range(span // tile):
            out, out_tangent = [
                jnp.dot(
                    picks[...],
                    returned[f, i, :, :, n * tile : (n + 1) * tile].reshape(NZ * CAP, tile),
                    preferred_element_type=F32,
                )
                for i in range(2)
            ]
            for i in range(tile // strip):
                at = (2 * (n * tile // strip + i) + f // (PARTS // 2)) * piece_rows + f % (PARTS // 2) * strip
                to, of = slice(at, at + strip), slice(i * strip, (i + 1) * strip)
                g0, g1, m0, m1 = [
                    jnp.concatenate([spread[j]] * (strip // n_tokens), axis=1) if strip > n_tokens else spread[j]
                    for j in range(4)
                ]
                y0, y1 = out[:n_tokens, of], out[n_tokens:, of]
                total = g0 * y0 + g1 * y1
                moved = (m0 * y0 + g0 * out_tangent[:n_tokens, of]) + (m1 * y1 + g1 * out_tangent[n_tokens:, of])
                mixed[:, to] = (tokens[:, to].astype(F32) + opened[:, to] * total).astype(BF16)
                mixed_tangent[:, to] = (
                    tangent[:, to].astype(F32) + opened_move[:, to] * total + opened[:, to] * moved
                ).astype(BF16)
                outs += [
                    pltpu.make_async_copy(a.at[:, to], b.at[:, to], out_sem.at[len(outs) + j])
                    for j, (a, b) in enumerate(((mixed, mixed_out), (mixed_tangent, mixed_tangent_out)))
                ]
                for out_copy in outs[-2:]:
                    out_copy.start()

    for out_copy in outs:
        out_copy.wait()
    wait(packed.at[0 : 2 * (GROUP - 1)], packed_sem)
    wait(results.at[:, :, 0 : GROUP - 1], results_sem)
    wait(weights.at[0, 0 : 12 * rc], right_sem)
    wait(weights.at[:, 0 : 12 * rc], side_sem)

    @pl.when(dr != 1)
    def _():
        wait(weights.at[1, 0 : 12 * rc], left_sem)

    @pl.when(source)
    def _():
        wait(own, seed_y)

    @pl.when(source & (c != taker))
    def _():
        wait(own, seed_core)


def body(
    tokens,
    token_tangent,
    mod_scale,
    mod_shift,
    scale_tangent,
    shift_tangent,
    out_gate,
    out_gate_tangent,
    routes,
    router_gates,
    router_tangents,
    gate_weight,
    up_weight,
    down_weight,
):
    n_tokens, width = tokens.shape
    _, piece_rows, inner = gate_weight.shape
    rc = piece_rows // CH
    shape = (rc, CH, inner)
    vmem, anywhere = pl.BlockSpec(memory_space=pltpu.VMEM), pl.BlockSpec(memory_space=pl.ANY)
    dma = pltpu.SemaphoreType.DMA
    slab = (2, CAP, width)
    return tuple(pl.pallas_call(
        moe_kernel,
        name="moe",
        out_shape=[jax.ShapeDtypeStruct(tokens.shape, BF16)] * 2,
        in_specs=[anywhere] * 2 + [vmem] * 9 + [anywhere] * 3,
        out_specs=[anywhere] * 2,
        scratch_shapes=[pltpu.VMEM(tokens.shape, BF16)] * 4
        + [
            dma((2,)),
            dma((2 * 2 * NY * 2,)),
            pltpu.VMEM((3, *shape), BF16),
            pltpu.VMEM((2, 3 * 2 * NY * rc, CH, inner), BF16),
            pltpu.VMEM((2, n_tokens, width), BF16),
            pltpu.VMEM((NZ * CAP, n_tokens), BF16),
            pltpu.VMEM((2 * n_tokens, NZ * CAP), BF16),
            pltpu.VMEM((4, n_tokens, n_tokens), F32),
            pltpu.VMEM((NZ, *slab), BF16),
            pltpu.VMEM((2, GROUP, *slab), BF16),
            pltpu.VMEM((2, GROUP, 2, CAP, inner), BF16),
            pltpu.VMEM((2, PARTS, GROUP, 2, CAP, width // PARTS), BF16),
            pltpu.VMEM((PARTS, 2, NZ, CAP, width // PARTS), BF16),
            dma((3,)),
            dma((2, 12 * rc)),
            dma((2, 1 + PARTS)),
            dma((2,)),
            dma((PARTS,)),
        ]
        + [dma] * 7,
        compiler_params=pltpu.CompilerParams(
            collective_id=0, has_side_effects=True, vmem_limit_bytes=60 * 2**20
        ),
    )(
        tokens,
        token_tangent,
        *[
            v.reshape(1, width)
            for v in (mod_scale, mod_shift, scale_tangent, shift_tangent, out_gate, out_gate_tangent)
        ],
        routes.T,
        router_gates.T,
        router_tangents.T,
        gate_weight.reshape(shape),
        up_weight.reshape(shape),
        down_weight.reshape(shape),
    ))


def solution(mesh):
    rows = P(("dp", "ctx", "expert"), None)
    expert_rows = P("expert", "ctx", None)
    in_specs = (rows,) * 2 + (P("dp"),) * 6 + (rows,) * 3 + (expert_rows,) * 3
    return jax.shard_map(body, mesh=mesh, in_specs=in_specs, out_specs=(rows, rows), check_vma=False)
```

```python
import jax
import jax.numpy as jnp
from jax import lax
from jax.experimental import pallas as pl
from jax.experimental.pallas import tpu as pltpu
from jax.sharding import PartitionSpec as P

MESH = pl.DeviceIdType.MESH
BF16, F32 = jnp.bfloat16, jnp.float32
NX, NY, NZ = 4, 4, 16
GROUP = 2 * NX
CAP = 32
CH = 32
JOIN = 2
HOP = 6
SIDE = 3
DEAL = 4
LEAD = 8
PARTS = 4


def mod(a, n):
    return lax.rem(a + 4 * n, n)


def moe_kernel(
    tokens_in, tangent_in, scale, shift, scale_move, shift_move, opened, opened_move,
    routes, gates, gate_moves, gate_w, up_w, down_w,
    mixed_out, mixed_tangent_out,
    tokens, tangent, mixed, mixed_tangent, row_sem, out_sem,
    own, weights, modded, slots, picks, spread, packed, rows, hidden, results, returned,
    own_sem, z_sem, y_sem, x_sem, back_sem,
    seed_core, seed_y, right_sem, left_sem, side_sem, packed_sem, results_sem,
):
    n_tokens, width = tokens.shape
    pieces = 2 * NY
    piece_rows = width // pieces
    rc = piece_rows // CH
    n_first = 4 * rc
    n_all = 6 * rc
    span = width // PARTS
    strip = span // NY
    tile = 256
    x, k, z = lax.axis_index("dp"), lax.axis_index("ctx"), lax.axis_index("expert")
    y, c = k >> 1, k & 1
    me = 2 * x + c

    def place(j):
        return (j >> 1, 2 * y + (j & 1), z)

    def right_distance(j):
        return mod(z - j - 1, 8) + 1

    def expert(j, s):
        return mod(z - right_distance(j) + 8 * s, NZ)

    dr = right_distance(me)
    source = ((z & 7) >> 1) == x
    taker = z & 1

    loads = [
        pltpu.make_async_copy(w, own.at[i], own_sem.at[i]) for i, w in enumerate((gate_w, up_w, down_w))
    ]
    loads += [
        pltpu.make_async_copy(a, b, row_sem.at[i])
        for i, (a, b) in enumerate(((tokens_in, tokens), (tangent_in, tangent)))
    ]
    for load in loads:
        load.start()

    barrier = pltpu.get_barrier_semaphore()
    peers = [(x, k, mod(z + 1, NZ)), (x, k, mod(z - 1, NZ))]
    for step in (1, -1):
        for core in range(2):
            peers.append((x, 2 * mod(y + step, NY) + core, z))
    for other in range(1, GROUP):
        peers.append(place(lax.rem(me + other, GROUP)))
    for peer in peers:
        pl.semaphore_signal(barrier, inc=1, device_id=peer, device_id_type=MESH)

    pl.semaphore_wait(barrier, len(peers))
    for load in loads[:3]:
        load.wait()

    def send(src, dst, send_sem, recv_sem, device):
        pltpu.make_async_remote_copy(
            src_ref=src, dst_ref=dst, send_sem=send_sem, recv_sem=recv_sem, device_id=device, device_id_type=MESH
        ).start()

    def wait(ref, sem):
        pltpu.make_async_copy(ref, ref, sem).wait()

    ahead, behind = mod(y + 1, NY), mod(y - 1, NY)
    lag = ((HOP * dr) >> 1, (HOP * (8 - dr)) >> 1)

    def decode(j):
        n, r = lax.div(j, rc), lax.rem(j, rc)
        return n >> 1, n & 1, r, (lax.div(r, JOIN) & 1) == 1

    def seed(j):
        mat, p, r, turned = decode(j)

        @pl.when(source & (j < n_all) & (p == c))
        def _():
            src = own.at[mat, r]
            dst = weights.at[1, (8 * mat + 2 * y + p) * rc + r]

            @pl.when(c == taker)
            def _():
                pltpu.make_async_copy(src, dst, z_sem.at[1, 2 * j]).start()

            @pl.when(c != taker)
            def _():
                send(src, dst, seed_core, z_sem.at[1, 2 * j], (x, 2 * y + taker, z))

            column = jnp.where(turned, behind, ahead)
            send(src, dst, seed_y, z_sem.at[1, 2 * j + 1], (x, 2 * column + taker, z))

    def step(t, s):
        j = t - lag[s]

        @pl.when((j >= 0) & (j < n_all))
        def _():
            mat, p, r, turned = decode(j)
            base = (8 * mat + p) * rc + r
            second = jnp.where(turned, ahead, behind)
            for a, column in enumerate((y, second)):
                row = base + 2 * rc * column
                block = weights.at[s, row]
                i = 2 * j + a
                wait(block, z_sem.at[s, i])

                @pl.when(dr < 8 if s == 0 else dr == 8)
                def _():
                    send(block, weights.at[0, row], right_sem, z_sem.at[0, i], (x, k, mod(z + 1, NZ)))

                if s == 1:

                    @pl.when(dr != 1)
                    def _():
                        send(block, weights.at[1, row], left_sem, z_sem.at[1, i], (x, k, mod(z - 1, NZ)))

            @pl.when(lax.rem(r, JOIN) == JOIN - 1)
            def _():
                part = jnp.where(mat < 2, 0, 1 + lax.div(j - n_first, 2 * rc // PARTS))
                for a, column in enumerate((y, second)):
                    joined = weights.at[s, pl.ds(base + 2 * rc * column - (JOIN - 1), JOIN)]
                    side = jnp.where(turned, behind, ahead) if a else second
                    send(joined, joined, side_sem, y_sem.at[s, part], (x, 2 * side + c, z))

    def first_products(s, n):
        @pl.when(n == 0)
        def _():
            wait(rows.at[s], x_sem.at[s])
            wait(weights.at[s, 0 : 8 * rc], y_sem.at[s, 0])

        few = tile // 2
        cols = pl.ds(pl.multiple_of(n * few, few), few)
        left = rows[s].reshape(GROUP * 2 * CAP, width)
        right = jnp.concatenate(
            [weights[s, i * 8 * rc : (i + 1) * 8 * rc, :, cols].reshape(width, few) for i in range(2)], axis=1
        )
        out = jnp.dot(left, right, preferred_element_type=F32).reshape(GROUP, 2, CAP, tile)
        u, du, v, dv = out[:, 0, :, :few], out[:, 1, :, :few], out[:, 0, :, few:], out[:, 1, :, few:]
        sigma = jax.nn.sigmoid(u)
        active = u * sigma
        slope = sigma * (1.0 + u * (1.0 - sigma))
        hidden[s, :, 0, :, cols] = (active * v).astype(BF16)
        hidden[s, :, 1, :, cols] = (slope * du * v + active * dv).astype(BF16)

    def second_products(s, f):
        wait(weights.at[s, 0 : 4 * rc // PARTS], y_sem.at[s, 1 + f])
        few = strip // CH
        start = (16 + lax.div(f, PARTS // 2)) * rc + lax.rem(f, PARTS // 2) * few
        left = hidden[s].reshape(GROUP * 2 * CAP, hidden.shape[-1])
        for n in range(span // tile):
            right = jnp.concatenate(
                [
                    weights[s, pl.ds(start + 2 * rc * i, few)].reshape(strip, hidden.shape[-1])
                    for i in range(n * tile // strip, (n + 1) * tile // strip)
                ],
                axis=0,
            )
            out = lax.dot_general(left, right, (((1,), (1,)), ((), ())), preferred_element_type=F32)
            results[s, f, :, :, :, n * tile : (n + 1) * tile] = out.astype(BF16).reshape(GROUP, 2, CAP, tile)

    def give(s, f, first):
        e = expert(me, s)

        @pl.when(first == 0)
        def _():
            pltpu.make_async_copy(results.at[s, f, me], returned.at[f, :, e], back_sem.at[f]).start()

        def one(other, _):
            j = (me + other) & (GROUP - 1)
            send(results.at[s, f, j], returned.at[f, :, e], results_sem, back_sem.at[f], place(j))
            return 0

        lax.fori_loop(jnp.maximum(first, 1), first + GROUP // 2, one, 0)

    def go_ahead(j, _):
        seed(j)
        return 0

    lax.fori_loop(0, LEAD, go_ahead, 0)

    def choose(i):
        sublanes = lax.broadcasted_iota(jnp.int32, (NZ, n_tokens), 0)
        named = [sublanes == routes[j : j + 1] for j in range(2)]
        before = lax.broadcasted_iota(jnp.int32, (n_tokens, n_tokens), 0) < lax.broadcasted_iota(
            jnp.int32, (n_tokens, n_tokens), 1
        )
        counts = jnp.dot(
            (named[0] | named[1]).astype(F32).astype(BF16),
            before.astype(F32).astype(BF16),
            preferred_element_type=F32,
        )
        places = lax.broadcasted_iota(jnp.int32, (NZ * CAP, n_tokens), 0)
        position = jnp.sum(jnp.where(named[i], counts, 0.0), axis=0, keepdims=True).astype(jnp.int32)
        taken = (places == routes[i : i + 1] * CAP + position).astype(F32)
        picks[i * n_tokens : (i + 1) * n_tokens] = taken.T.astype(BF16)
        slots[...] = taken.astype(BF16) if i == 0 else slots[...] + taken.astype(BF16)
        weight = (gates, gate_moves)[i]
        for j in range(2):
            spread[2 * i + j] = jnp.broadcast_to(weight[j : j + 1], (n_tokens, n_tokens)).T

    def modulate(n):
        at = pl.ds(pl.multiple_of(n * 32, 32), 32)
        primal, moving = tokens[at].astype(F32), tangent[at].astype(F32)
        inverse = lax.rsqrt(jnp.mean(primal * primal, axis=-1, keepdims=True) + 1e-06)
        normed = primal * inverse
        normed_tangent = (moving - normed * jnp.mean(normed * moving, axis=-1, keepdims=True)) * inverse
        widened = 1.0 + scale[...]
        modded[0, at] = (normed * widened + shift[...]).astype(BF16)
        modded[1, at] = (normed_tangent * widened + normed * scale_move[...] + shift_move[...]).astype(BF16)

    def deal(g):
        dealt = []
        for i in range(DEAL):
            n = DEAL * g + i
            j = (me + n) & (GROUP - 1)
            near = jnp.where(right_distance(j) <= 4, 0, 1)
            s = jnp.where(n < GROUP, near, 1 - near)
            dealt.append((n, j, s, expert(j, s)))
        chosen = jnp.concatenate(
            [slots[pl.ds(pl.multiple_of(e * CAP, CAP), CAP)] for _, _, _, e in dealt], axis=0
        )
        for at in range(0, width, 2 * tile):
            cols = slice(at, at + 2 * tile)
            for i in range(2):
                out = jnp.dot(chosen, modded[i, :, cols], preferred_element_type=F32)
                packed[pl.ds(DEAL * g, DEAL), i, :, cols] = out.astype(BF16).reshape(DEAL, CAP, 2 * tile)
        for i, (n, j, s, _) in enumerate(dealt):
            if i == 0:

                @pl.when(j == me)
                def _(n=n, s=s):
                    pltpu.make_async_copy(packed.at[n], rows.at[s, me], x_sem.at[s]).start()

                @pl.when(j != me)
                def _(n=n, s=s, j=j):
                    send(packed.at[n], rows.at[s, me], packed_sem, x_sem.at[s], place(j))

            else:
                send(packed.at[n], rows.at[s, me], packed_sem, x_sem.at[s], place(j))

    def turn(t, _):
        seed(t + LEAD)
        step(t, 0)
        step(t, 1)

        for i in range(2):

            @pl.when(t == i)
            def _(i=i):
                choose(i)
                loads[3 + i].wait()

        @pl.when((t >= 2) & (t < 4))
        def _():
            modulate(2 * t - 4)
            modulate(2 * t - 3)

        @pl.when((t >= 4) & (t < 4 + 2 * GROUP // DEAL))
        def _():
            deal(t - 4)

        def stream(s, _):
            u = t - jnp.where(s == 0, lag[0], lag[1]) - SIDE - n_first
            n_cols = 2 * hidden.shape[-1] // tile

            @pl.when((u >= 0) & (u < n_cols))
            def _():
                first_products(s, u)

            part_steps = 2 * rc // PARTS
            f = lax.div(u, part_steps) - 1
            at = lax.rem(u, part_steps)

            @pl.when((f >= 0) & (f < PARTS))
            def _():
                @pl.when(at == 0)
                def _():
                    second_products(s, f)

                @pl.when(at < 2)
                def _():
                    give(s, f, at * (GROUP // 2))

            return 0

        lax.fori_loop(0, 2, stream, 0)
        return 0

    lax.fori_loop(0, n_all + 4 * HOP + SIDE + 2, turn, 0)

    outs = []
    for f in range(PARTS):
        wait(returned.at[f], back_sem.at[f])
        for n in range(span // tile):
            out, out_tangent = [
                jnp.dot(
                    picks[...],
                    returned[f, i, :, :, n * tile : (n + 1) * tile].reshape(NZ * CAP, tile),
                    preferred_element_type=F32,
                )
                for i in range(2)
            ]
            for i in range(tile // strip):
                at = (2 * (n * tile // strip + i) + f // (PARTS // 2)) * piece_rows + f % (PARTS // 2) * strip
                to, of = slice(at, at + strip), slice(i * strip, (i + 1) * strip)
                g0, g1, m0, m1 = [
                    jnp.concatenate([spread[j]] * (strip // n_tokens), axis=1) if strip > n_tokens else spread[j]
                    for j in range(4)
                ]
                y0, y1 = out[:n_tokens, of], out[n_tokens:, of]
                total = g0 * y0 + g1 * y1
                moved = (m0 * y0 + g0 * out_tangent[:n_tokens, of]) + (m1 * y1 + g1 * out_tangent[n_tokens:, of])
                mixed[:, to] = (tokens[:, to].astype(F32) + opened[:, to] * total).astype(BF16)
                mixed_tangent[:, to] = (
                    tangent[:, to].astype(F32) + opened_move[:, to] * total + opened[:, to] * moved
                ).astype(BF16)
                outs += [
                    pltpu.make_async_copy(a.at[:, to], b.at[:, to], out_sem.at[len(outs) + j])
                    for j, (a, b) in enumerate(((mixed, mixed_out), (mixed_tangent, mixed_tangent_out)))
                ]
                for out_copy in outs[-2:]:
                    out_copy.start()

    for out_copy in outs:
        out_copy.wait()
    wait(packed.at[0 : 2 * (GROUP - 1)], packed_sem)
    wait(results.at[:, :, 0 : GROUP - 1], results_sem)
    wait(weights.at[0, 0 : 12 * rc], right_sem)
    wait(weights.at[:, 0 : 12 * rc], side_sem)

    @pl.when(dr != 1)
    def _():
        wait(weights.at[1, 0 : 12 * rc], left_sem)

    @pl.when(source)
    def _():
        wait(own, seed_y)

    @pl.when(source & (c != taker))
    def _():
        wait(own, seed_core)


def body(
    tokens,
    token_tangent,
    mod_scale,
    mod_shift,
    scale_tangent,
    shift_tangent,
    out_gate,
    out_gate_tangent,
    routes,
    router_gates,
    router_tangents,
    gate_weight,
    up_weight,
    down_weight,
):
    n_tokens, width = tokens.shape
    _, piece_rows, inner = gate_weight.shape
    rc = piece_rows // CH
    shape = (rc, CH, inner)
    vmem, anywhere = pl.BlockSpec(memory_space=pltpu.VMEM), pl.BlockSpec(memory_space=pl.ANY)
    dma = pltpu.SemaphoreType.DMA
    slab = (2, CAP, width)
    return tuple(pl.pallas_call(
        moe_kernel,
        name="moe",
        out_shape=[jax.ShapeDtypeStruct(tokens.shape, BF16)] * 2,
        in_specs=[anywhere] * 2 + [vmem] * 9 + [anywhere] * 3,
        out_specs=[anywhere] * 2,
        scratch_shapes=[pltpu.VMEM(tokens.shape, BF16)] * 4
        + [
            dma((2,)),
            dma((2 * 2 * NY * 2,)),
            pltpu.VMEM((3, *shape), BF16),
            pltpu.VMEM((2, 3 * 2 * NY * rc, CH, inner), BF16),
            pltpu.VMEM((2, n_tokens, width), BF16),
            pltpu.VMEM((NZ * CAP, n_tokens), BF16),
            pltpu.VMEM((2 * n_tokens, NZ * CAP), BF16),
            pltpu.VMEM((4, n_tokens, n_tokens), F32),
            pltpu.VMEM((NZ, *slab), BF16),
            pltpu.VMEM((2, GROUP, *slab), BF16),
            pltpu.VMEM((2, GROUP, 2, CAP, inner), BF16),
            pltpu.VMEM((2, PARTS, GROUP, 2, CAP, width // PARTS), BF16),
            pltpu.VMEM((PARTS, 2, NZ, CAP, width // PARTS), BF16),
            dma((3,)),
            dma((2, 12 * rc)),
            dma((2, 1 + PARTS)),
            dma((2,)),
            dma((PARTS,)),
        ]
        + [dma] * 7,
        compiler_params=pltpu.CompilerParams(
            collective_id=0, has_side_effects=True, vmem_limit_bytes=60 * 2**20
        ),
    )(
        tokens,
        token_tangent,
        *[
            v.reshape(1, width)
            for v in (mod_scale, mod_shift, scale_tangent, shift_tangent, out_gate, out_gate_tangent)
        ],
        routes.T,
        router_gates.T,
        router_tangents.T,
        gate_weight.reshape(shape),
        up_weight.reshape(shape),
        down_weight.reshape(shape),
    ))


def solution(mesh):
    rows = P(("dp", "ctx", "expert"), None)
    expert_rows = P("expert", "ctx", None)
    in_specs = (rows,) * 2 + (P("dp"),) * 6 + (rows,) * 3 + (expert_rows,) * 3
    return jax.shard_map(body, mesh=mesh, in_specs=in_specs, out_specs=(rows, rows), check_vma=False)
```
